512 devices in a mesh: flop: 64 (over z, y), turn: 8 (over x, core).
Axes of the slice: x: 4, y: 4, z: 16, core: 2. Of those that a mesh axis runs over, the one named last changes fastest.
Arguments:
- root_reach: float32 [2, 1326], replicated, may hold values from 0.05 to 1
- stakes: float32 [5, 5], replicated, may hold values from 0.005 to 0.05
- flop_regrets: float32 [64, 5, 1326], P('flop'), may hold values from 0.1 to 1
- turn_regrets: float32 [64, 5, 32, 5, 1326], P('flop', None, 'turn'), may hold values from 0.1 to 1
- flop_cards: int32 [64, 3], P('flop'), may hold values from 0 to 51, as said below
- turn_cards: int32 [64, 32], P('flop', 'turn'), may hold values from 0 to 51, as said below
- river_cards: int32 [64, 32, 8], P('flop', 'turn'), may hold values from 0 to 51, as said below
- hand_ranks: int32 [64, 32, 8, 1326], P('flop', 'turn'), may hold values from 0 to 7461
- board_count: int32 [64, 8], P('flop', 'turn'), may hold values from 8 to 32, as said below
Outputs:
- flop_next: float32 [64, 5, 1326], P('flop')
- turn_next: float32 [64, 5, 32, 5, 1326], P('flop', None, 'turn')
- root_values: float32 [2, 1326], replicated
The draws below stay inside these ranges and needn't reach their ends.
Inputs may be any that keep to these rules, and one draw needn't show every extreme that they name: `flop_cards`: for each flop, its three flop cards, its 32 turn cards and the 8 river cards of any one of its turn cards are all different cards. `turn_cards`: different cards within one flop, none of them a flop card of that flop. `river_cards`: the 8 river cards of one turn card differ from each other, from that turn card and from the flop's cards. board_count[f, g] + board_count[(f + 32) mod 64, g] = 40 for every f and g.
All inputs are finite; a program needn't handle non-finite values.
Results may differ from the reference program's by a relative error of at most 0.0003.
Values may be sent and summed in bfloat16 or wider, within the bound.
No kernel may reach another device: no remote copies, remote signals or barrier semaphores. Data moves between devices by JAX's collectives and lax.ppermute only.
A program may use at most 64 MiB of HBM per device.

```python
import math
import jax
import jax.numpy as jnp
import numpy as np
from jax import lax

H = 1326
A = 5
TURN_DEV = 4
RIV = 8
FLOPS = 64
TURNS = 32
CAP = 32
SURPLUS = 12
BAL = 20
N_TURN = 8


def dealing(key):
    flop_keys = jax.random.split(key, FLOPS)
    shuffled = jax.vmap(lambda single: jax.random.permutation(single, 52))(flop_keys).astype(jnp.int32)
    river_index = 3 + TURNS + (jnp.arange(TURNS, dtype=jnp.int32)[:, None] * RIV + jnp.arange(RIV, dtype=jnp.int32)[None, :]) % (49 - TURNS)
    return (shuffled[:, :3], shuffled[:, 3:3 + TURNS], shuffled[:, river_index])


def draw_flop_cards(key, part):
    cards = dealing(key)
    return cards[0]


def draw_turn_cards(key, part):
    cards = dealing(key)
    return cards[1]


def draw_river_cards(key, part):
    cards = dealing(key)
    return cards[2]


def draw_board_count(key, part):
    key = jax.random.fold_in(key, 11)
    key_counts, key_forced, key_flip = jax.random.split(key, 3)
    halfway = FLOPS // 2
    lower = jax.random.randint(key_counts, (halfway * N_TURN,), BAL - SURPLUS, CAP + 1).astype(jnp.int32)
    forced = jax.random.randint(key_forced, (), 0, halfway * N_TURN).astype(jnp.int32)
    lower = jnp.where(jnp.arange(halfway * N_TURN, dtype=jnp.int32) == forced, CAP, lower)
    flipped = jax.random.randint(key_flip, (), 0, 2).astype(jnp.int32)
    lower = jnp.where(flipped == 1, 2 * BAL - lower, lower).reshape(halfway, N_TURN)
    return jnp.concatenate([lower, 2 * BAL - lower], axis=0).astype(jnp.int32)


def plant(drawn, rng, least, top_value):
    shape = drawn.shape
    spot = [jax.random.randint(jax.random.fold_in(rng, axis), (), 0, shape[axis]) for axis in range(len(shape))]
    drawn = drawn.at[tuple(spot)].set(least)
    longest = shape.index(max(shape))
    spot[longest] = (spot[longest] + 1) % shape[longest]
    return drawn.at[tuple(spot)].set(top_value)


def block_levels(own_key, extent, cuts, least, largest):
    def one(position, shards_of):
        heights = jax.random.uniform(jax.random.fold_in(jax.random.fold_in(own_key, 6), position), (shards_of,), jnp.float32, least / len(cuts), largest / len(cuts))
        return jnp.repeat(jnp.exp(heights), extent[position] // shards_of).reshape((-1,) + (1,) * (len(extent) - position - 1))

    factor_of = one(*cuts[0])
    for cut in cuts[1:]:
        factor_of = factor_of * one(*cut)
    return factor_of


def setup_inputs(seed: int = 0) -> dict:
    keys = jax.random.split(jax.random.key(seed), 10)
    return {
        "root_reach": jnp.clip(jax.random.uniform(keys[0], (2, H), jnp.float32, 0.05, 1.0), 0.05, 1.0),
        "stakes": jnp.clip(jnp.exp(jax.random.uniform(keys[1], (A, A), jnp.float32, math.log(0.005), math.log(0.05))), 0.005, 0.05),
        "flop_regrets": jnp.clip(0.1 + 0.9 * jax.random.uniform(keys[2], (FLOPS, A, H), jnp.float32) ** block_levels(keys[2], (FLOPS, A, H), ((0, 64),), -0.2, 0.2), 0.1, 1.0),
        "turn_regrets": jnp.clip(0.1 + 0.9 * jax.random.uniform(keys[3], (FLOPS, A, TURNS, A, H), jnp.float32) ** block_levels(keys[3], (FLOPS, A, TURNS, A, H), ((0, 64), (2, 8)), -0.2, 0.2), 0.1, 1.0),
        "flop_cards": draw_flop_cards(jax.random.fold_in(keys[9], 71), 0),
        "turn_cards": draw_turn_cards(jax.random.fold_in(keys[9], 71), 0),
        "river_cards": draw_river_cards(jax.random.fold_in(keys[9], 71), 0),
        "hand_ranks": plant(jax.random.randint(keys[7], (FLOPS, TURNS, RIV, H), 0, 7462), jax.random.fold_in(keys[7], 1), 0, 7461).astype(jnp.int32),
        "board_count": draw_board_count(jax.random.fold_in(keys[9], 71), 0),
    }


def hand_tables():
    low_np, high_np = np.triu_indices(52, 1)
    return jnp.asarray(low_np.astype(np.int32)), jnp.asarray(high_np.astype(np.int32))


def avoiding(low_card, high_card, cards):
    picked = cards[..., None]
    return ((low_card != picked) & (high_card != picked)).astype(jnp.float32)


def reference(root_reach, stakes, flop_regrets, turn_regrets, flop_cards, turn_cards, river_cards, hand_ranks, board_count):
    low_card, high_card = hand_tables()
    actions = flop_regrets.shape[1]
    hands = flop_regrets.shape[2]
    sharing = (low_card[:, None] == low_card[None, :]) | (low_card[:, None] == high_card[None, :])
    sharing = sharing | (high_card[:, None] == low_card[None, :]) | (high_card[:, None] == high_card[None, :])

    def board_sums(board_item):
        columns, ranks = board_item
        table = jnp.where(sharing, 0.0, jnp.sign(ranks[:, None] - ranks[None, :]).astype(jnp.float32))
        product = jnp.dot(columns.astype(jnp.float32), table.T, precision=lax.Precision.HIGHEST, preferred_element_type=jnp.float32)
        return jnp.concatenate([product[actions:], product[:actions]], axis=0)

    def per_flop(flop_data):
        flop_reg, turn_reg, flop_board, turn_board, river_board, ranks, counts = flop_data
        flop_mask = avoiding(low_card, high_card, flop_board[0]) * avoiding(low_card, high_card, flop_board[1]) * avoiding(low_card, high_card, flop_board[2])
        turn_mask = avoiding(low_card, high_card, turn_board)
        river_mask = avoiding(low_card, high_card, river_board)
        flop_policy = flop_reg / jnp.sum(flop_reg, axis=0, keepdims=True)
        turn_policy = turn_reg / jnp.sum(turn_reg, axis=2, keepdims=True)
        turn_index = jnp.arange(TURNS, dtype=jnp.int32)
        slot_index = (turn_index % TURN_DEV)[:, None] * RIV + jnp.arange(RIV, dtype=jnp.int32)[None, :]
        live = (slot_index < counts[turn_index // TURN_DEV][:, None]).astype(jnp.float32)
        reach_zero = root_reach[0] * flop_mask
        reach_one = root_reach[1] * flop_mask
        zero_cols = (((reach_zero[None, :] * flop_policy)[None, None] * turn_mask[:, None, None, :]) * river_mask[:, :, None, :]).astype(jnp.bfloat16)
        one_base = reach_one[None, :] * turn_mask
        one_prod = one_base[None, :, None, :] * turn_policy
        one_mix = jnp.transpose(jnp.sum(stakes[:, None, :, None] * one_prod, axis=2), (1, 0, 2))
        one_cols = (one_mix[:, None] * river_mask[:, :, None, :]).astype(jnp.bfloat16)
        columns = jnp.concatenate([zero_cols, one_cols], axis=2)
        columns = columns.reshape(TURNS * RIV, 2 * actions, hands)
        results = lax.map(board_sums, (columns, ranks.reshape(TURNS * RIV, hands)))
        results = results.reshape(TURNS, RIV, 2 * actions, hands)
        weight = ((flop_mask[None, None, :] * turn_mask[:, None, :]) * river_mask) * live[:, :, None]
        zero_turn = jnp.sum(results[:, :, :actions] * weight[:, :, None, :], axis=1) / RIV
        one_mean = jnp.sum(results[:, :, actions:] * weight[:, :, None, :], axis=1) / RIV
        one_action = stakes[:, None, :, None] * jnp.transpose(one_mean, (1, 0, 2))[:, :, None, :]
        one_turn = jnp.sum(turn_policy * one_action, axis=2)
        turn_new = jnp.maximum(turn_reg + one_action - one_turn[:, :, None, :], 0.0)
        zero_action = jnp.sum(zero_turn, axis=0) / TURNS
        one_flop = jnp.sum(one_turn, axis=(0, 1)) / TURNS
        zero_flop = jnp.sum(flop_policy * zero_action, axis=0)
        flop_new = jnp.maximum(flop_reg + zero_action - zero_flop, 0.0)
        return flop_new, turn_new, zero_flop, one_flop

    flop_next, turn_next, zero_all, one_all = lax.map(per_flop, (flop_regrets, turn_regrets, flop_cards, turn_cards, river_cards, hand_ranks, board_count))
    root_values = jnp.stack([jnp.sum(zero_all, axis=0), jnp.sum(one_all, axis=0)])
    return flop_next, turn_next, root_values
```

```python
import jax
import jax.numpy as jnp
import numpy as np
from jax import lax
from jax.experimental import pallas as pl
from jax.experimental.pallas import tpu as pltpu
from jax.sharding import PartitionSpec as P

HANDS = 1326
ROWS = 1328
WIDTH = 1408
CHUNK = 256
UNROLL = 4
TURNS_ALL = 32


def hand_tables():
    low, high = np.triu_indices(52, 1)
    cards = np.full((2, WIDTH), 99, np.int32)
    cards[0, :HANDS] = low
    cards[1, :HANDS] = high
    share = (low[:, None] == low[None, :]) | (low[:, None] == high[None, :])
    share |= (high[:, None] == low[None, :]) | (high[:, None] == high[None, :])
    apart = np.zeros((ROWS, WIDTH), np.float32)
    apart[:HANDS, :HANDS] = ~share
    return cards, apart


def avoid(low, high, card):
    return jnp.where((low != card) & (high != card), 1.0, 0.0)


def iteration_kernel(
    flop_cards_hbm,
    turn_cards_hbm,
    river_cards_hbm,
    board_count_hbm,
    stakes_hbm,
    reach_hbm,
    flop_reg_hbm,
    turn_reg_hbm,
    ranks_hbm,
    cards_hbm,
    apart_hbm,
    mean_out,
    share,
    flop_cards,
    turn_cards,
    river_cards,
    board_count,
    stakes,
    reach,
    flop_reg,
    turn_reg,
    ranks,
    cards,
    apart,
    columns,
    keys,
    keys_t,
    worth,
    sums,
    arrived,
):
    actions = flop_reg.shape[0]
    turns = turn_reg.shape[2]
    boards = ranks.shape[0]
    rivers = boards // turns
    pairs = (
        (ranks_hbm, ranks),
        (cards_hbm, cards),
        (flop_cards_hbm, flop_cards),
        (turn_cards_hbm, turn_cards),
        (river_cards_hbm, river_cards),
        (board_count_hbm, board_count),
        (stakes_hbm, stakes),
        (reach_hbm, reach),
        (flop_reg_hbm, flop_reg),
        (turn_reg_hbm, turn_reg),
        (apart_hbm, apart),
    )
    copies = [
        pltpu.make_async_copy(source, held, arrived.at[spot])
        for spot, (source, held) in enumerate(pairs)
    ]
    for copy in copies:
        copy.start()

    keys[...] = jnp.zeros(keys.shape, jnp.float32)
    columns[...] = jnp.zeros(columns.shape, jnp.float32)
    sums[...] = jnp.zeros(sums.shape, jnp.float32)
    copies[0].wait()
    drawn = ranks[...]
    power = jnp.exp2((drawn >> 7).astype(jnp.float32))
    mantissa = ((drawn & 127) + 128).astype(jnp.float32)
    keys[:boards, :HANDS] = power * mantissa
    for part in range(WIDTH // 128):
        lanes = slice(part * 128, (part + 1) * 128)
        keys_t[lanes, :] = keys[:, lanes].T
    for copy in copies[1:10]:
        copy.wait()

    low = cards[0:1, :]
    high = cards[1:2, :]
    low_h = cards[0:1, :HANDS]
    high_h = cards[1:2, :HANDS]
    flop_mask = (
        avoid(low_h, high_h, flop_cards[0, 0])
        * avoid(low_h, high_h, flop_cards[0, 1])
        * avoid(low_h, high_h, flop_cards[0, 2])
    )
    turn_mask = jnp.concatenate(
        [avoid(low_h, high_h, turn_cards[0, t]) for t in range(turns)], axis=0
    )
    total = flop_reg[0]
    for a in range(1, actions):
        total = total + flop_reg[a]
    reach_zero = reach[0:1, :] * flop_mask
    for a in range(actions):
        column = reach_zero * (flop_reg[a] / total)
        for t in range(turns):
            columns[t, a : a + 1, :HANDS] = column * turn_mask[t : t + 1, :]
    base = (reach[1:2, :] * flop_mask) * turn_mask
    for a in range(actions):
        total = turn_reg[a, 0]
        for b in range(1, actions):
            total = total + turn_reg[a, b]
        mix = None
        gain = None
        for b in range(actions):
            chance = turn_reg[a, b] / total
            term = stakes[a, b] * (base * chance)
            mix = term if mix is None else mix + term
            term = stakes[a, b] * chance
            gain = term if gain is None else gain + term
        worth[a] = gain
        for t in range(turns):
            columns[t, actions + a : actions + a + 1, :HANDS] = mix[t : t + 1, :]
    copies[10].wait()
    live_count = board_count[0, 0]

    def some_boards(step, carry):
        first = step * UNROLL
        t = first // rivers
        gathered = None
        for ahead in range(UNROLL):
            board = first + ahead
            river_mask = avoid(low, high, river_cards[t, board % rivers])
            mixed = (columns[t] * river_mask).astype(jnp.bfloat16)
            row = keys[pl.ds(board, 1), :].astype(jnp.bfloat16)
            out = None
            for start in range(0, ROWS, CHUNK):
                size = min(CHUNK, ROWS - start)
                rows = slice(start, start + size)
                picked = jnp.full((size, 128), board, jnp.int32)
                column = jnp.take_along_axis(keys_t[rows, :], picked, axis=1)
                column = column.astype(jnp.bfloat16)
                column = jnp.concatenate([column] * (WIDTH // 128), axis=1)
                table = jnp.clip(row - column, -1.0, 1.0) * apart[rows, :]
                part = jnp.dot(mixed[:, rows], table, preferred_element_type=jnp.float32)
                out = part if out is None else out + part
            live = jnp.where(board < live_count, 1.0, 0.0)
            out = out * (river_mask * live)
            gathered = out if gathered is None else gathered + out
        sums[t] = sums[t] + gathered
        return carry

    lax.fori_loop(0, (live_count + (UNROLL - 1)) // UNROLL, some_boards, 0)

    turns_all = TURNS_ALL * 1.0
    zero = None
    for t in range(turns):
        term = sums[t, actions : 2 * actions, :HANDS] * (
            flop_mask * turn_mask[t : t + 1, :]
        )
        zero = term if zero is None else zero + term
    share[0:actions, :] = zero / (rivers * turns_all)
    one_share = None
    for a in range(actions):
        mean = jnp.concatenate([sums[t, a : a + 1, :HANDS] for t in range(turns)], axis=0)
        mean = mean * (flop_mask * turn_mask) / rivers
        mean_out[a] = mean
        node = worth[a] * mean
        one_share = node if one_share is None else one_share + node
    share[actions : actions + 1, :] = jnp.sum(one_share, axis=0, keepdims=True) / turns_all


def iterate(flop_cards, turn_cards, river_cards, board_count, stakes, reach, flop_reg, turn_reg, ranks):
    actions, _, hands = flop_reg.shape
    turns = turn_reg.shape[2]
    cards, apart = hand_tables()
    vmem = pl.BlockSpec(memory_space=pltpu.VMEM)
    operands = (
        flop_cards,
        turn_cards,
        river_cards,
        board_count,
        stakes,
        reach,
        flop_reg,
        turn_reg,
        ranks,
        jnp.asarray(cards),
        jnp.asarray(apart.astype(jnp.bfloat16)),
    )
    return pl.pallas_call(
        iteration_kernel,
        out_shape=(
            jax.ShapeDtypeStruct((actions, turns, hands), jnp.float32),
            jax.ShapeDtypeStruct((actions + 1, hands), jnp.float32),
        ),
        in_specs=[pl.BlockSpec(memory_space=pltpu.HBM)] * len(operands),
        out_specs=(vmem, vmem),
        scratch_shapes=[pltpu.SMEM(held.shape, held.dtype) for held in operands[:5]]
        + [pltpu.VMEM(held.shape, held.dtype) for held in operands[5:]]
        + [
            pltpu.VMEM((turns, 16, WIDTH), jnp.float32),
            pltpu.VMEM((128, WIDTH), jnp.float32),
            pltpu.VMEM((WIDTH, 128), jnp.float32),
            pltpu.VMEM((actions, turns, hands), jnp.float32),
            pltpu.VMEM((turns, 16, WIDTH), jnp.float32),
            pltpu.SemaphoreType.DMA((len(operands),)),
        ],
        compiler_params=pltpu.CompilerParams(vmem_limit_bytes=62 * 1024 * 1024),
        cost_estimate=pl.CostEstimate(
            flops=32 * 2 * 16 * HANDS * HANDS, bytes_accessed=5000000, transcendentals=0
        ),
        name="iteration",
    )(*operands)


def regret_kernel(stakes, mean, turn_reg, turn_next):
    actions = turn_reg.shape[0]
    for a in range(actions):
        total = turn_reg[a, 0]
        for b in range(1, actions):
            total = total + turn_reg[a, b]
        values = [stakes[a, b] * mean[a] for b in range(actions)]
        node = None
        for b in range(actions):
            term = (turn_reg[a, b] / total) * values[b]
            node = term if node is None else node + term
        for b in range(actions):
            turn_next[a, b] = jnp.maximum(turn_reg[a, b] + values[b] - node, 0.0)


def updated(stakes, mean, turn_reg):
    vmem = pl.BlockSpec(memory_space=pltpu.VMEM)
    return pl.pallas_call(
        regret_kernel,
        out_shape=jax.ShapeDtypeStruct(turn_reg.shape, jnp.float32),
        in_specs=[pl.BlockSpec(memory_space=pltpu.SMEM), vmem, vmem],
        out_specs=vmem,
        cost_estimate=pl.CostEstimate(flops=2000000, bytes_accessed=1200000, transcendentals=0),
        name="turn_regrets",
    )(stakes, mean, turn_reg)


def summed(block, axis, groups=None):
    count = lax.axis_size(axis) if groups is None else len(groups[0])
    spread = jnp.broadcast_to(block[None], (count,) + block.shape)
    heard = lax.all_to_all(spread, axis, 0, 0, axis_index_groups=groups, tiled=True)
    return jnp.sum(heard, axis=0)


def tiled(rows):
    count = rows.size
    padded = -(-count // 1024) * 1024
    return jnp.pad(rows.reshape(-1), (0, padded - count)).reshape(-1, 128)


def per_device(
    root_reach,
    stakes,
    flop_regrets,
    turn_regrets,
    flop_cards,
    turn_cards,
    river_cards,
    hand_ranks,
    board_count,
):
    actions = flop_regrets.shape[1]
    hands = flop_regrets.shape[2]
    turns = turn_cards.shape[1]
    rivers = river_cards.shape[2]
    flop_reg = jnp.transpose(flop_regrets, (1, 0, 2))
    turn_reg = jnp.transpose(turn_regrets[0], (0, 2, 1, 3))
    mean, share = iterate(
        flop_cards,
        turn_cards,
        river_cards[0],
        board_count,
        stakes,
        root_reach,
        flop_reg,
        turn_reg,
        hand_ranks.reshape(turns * rivers, hands),
    )
    turn_new = updated(stakes, mean, turn_reg)
    total = summed(tiled(share), "turn").reshape(-1)[: share.size].reshape(share.shape)
    regrets = flop_regrets[0]
    flop_policy = regrets / jnp.sum(regrets, axis=0, keepdims=True)
    zero_action = total[:actions]
    zero_flop = jnp.sum(flop_policy * zero_action, axis=0)
    flop_next = jnp.maximum(regrets + zero_action - zero_flop, 0.0)[None]
    values = tiled(jnp.stack([zero_flop, total[actions]]))
    values, flop_next, turn_new = lax.optimization_barrier((values, flop_next, turn_new))
    turn_next = jnp.transpose(turn_new, (0, 2, 1, 3))[None]
    flops = lax.axis_size("flop")
    near = [list(range(i, i + 4)) for i in range(0, flops, 4)]
    far = [list(range(i, flops, 4)) for i in range(4)]
    values = summed(summed(values, "flop", near), "flop", far)
    root_values = values.reshape(-1)[: 2 * hands].reshape(2, hands)
    return (flop_next, turn_next, root_values)


def solution(mesh):
    in_specs = (
        P(),
        P(),
        P("flop", None, None),
        P("flop", None, "turn", None, None),
        P("flop", None),
        P("flop", "turn"),
        P("flop", "turn", None),
        P("flop", "turn", None, None),
        P("flop", "turn"),
    )
    out_specs = (P("flop", None, None), P("flop", None, "turn", None, None), P())
    return jax.shard_map(
        per_device, mesh=mesh, in_specs=in_specs, out_specs=out_specs, check_vma=False
    )
```

```python
import jax
import jax.numpy as jnp
import numpy as np
from jax import lax
from jax.experimental import pallas as pl
from jax.experimental.pallas import tpu as pltpu
from jax.sharding import PartitionSpec as P

HANDS = 1326
WIDTH = 1408
DECK = 48
LIVE = 1128
ROWS = 1136
SPAN = 1152
SHIFTS = 8
CHUNK = 256
UNROLL = 8
TURNS_ALL = 32
DEVICES = 8
LINES = 72


def hand_tables():
    low, high = np.triu_indices(52, 1)
    cards = np.full((2, WIDTH), 99, np.int32)
    cards[0, :HANDS] = low
    cards[1, :HANDS] = high
    low, high = np.triu_indices(DECK, 1)
    share = (low[:, None] == low[None, :]) | (low[:, None] == high[None, :])
    share |= (high[:, None] == low[None, :]) | (high[:, None] == high[None, :])
    apart = np.zeros((ROWS, SPAN), np.float32)
    apart[:LIVE, :LIVE] = ~share
    return cards, apart


def avoid(low, high, card):
    return jnp.where((low != card) & (high != card), 1.0, 0.0)


def below(card, cards):
    count = (card > cards[0]).astype(jnp.int32)
    for other in cards[1:]:
        count = count + (card > other).astype(jnp.int32)
    return count


def iteration_kernel(
    flop_cards_hbm,
    turn_cards_hbm,
    river_cards_hbm,
    board_count_hbm,
    stakes_hbm,
    cards_hbm,
    ranks_hbm,
    reach_hbm,
    flop_reg_hbm,
    turn_reg_hbm,
    apart_hbm,
    mean_out,
    message,
    flop_cards,
    turn_cards,
    river_cards,
    board_count,
    stakes,
    cards,
    ranks,
    reach,
    flop_reg,
    turn_reg,
    apart,
    wide,
    moves,
    arrivals,
    keys,
    keys_t,
    columns,
    worth,
    sums,
    others,
    lines,
    arrived,
):
    actions = flop_reg.shape[0]
    turns = turn_reg.shape[2]
    boards = ranks.shape[0]
    rivers = boards // turns
    pairs = (
        (flop_cards_hbm, flop_cards),
        (turn_cards_hbm, turn_cards),
        (river_cards_hbm, river_cards),
        (board_count_hbm, board_count),
        (stakes_hbm, stakes),
        (cards_hbm, cards),
        (ranks_hbm, ranks),
        (reach_hbm, reach),
        (flop_reg_hbm, flop_reg),
        (turn_reg_hbm, turn_reg),
        (apart_hbm, apart),
    )
    copies = [
        pltpu.make_async_copy(source, held, arrived.at[spot])
        for spot, (source, held) in enumerate(pairs)
    ]
    for copy in copies:
        copy.start()

    tail = slice(WIDTH - 128, WIDTH)
    wide[:, :, tail] = jnp.zeros((turns + 1, 16, 128), jnp.float32)
    sums[...] = jnp.zeros(sums.shape, jnp.float32)
    lines[...] = jnp.zeros(lines.shape, jnp.float32)
    for t in range(turns):
        columns[t, 8:16, :] = jnp.zeros((8, SPAN), jnp.float32)
    for copy in copies[:6]:
        copy.wait()

    shape = (2 * turns, WIDTH)
    low = jnp.broadcast_to(cards[0:1, :], shape)
    high = jnp.broadcast_to(cards[1:2, :], shape)
    place = lax.broadcasted_iota(jnp.int32, shape, 1)
    which = lax.broadcasted_iota(jnp.int32, shape, 0) >> 1
    turn_card = jnp.full(shape, turn_cards[0, 0], jnp.int32)
    for t in range(1, turns):
        turn_card = jnp.where(which == t, turn_cards[0, t], turn_card)
    gone = [flop_cards[0, 0], flop_cards[0, 1], flop_cards[0, 2], turn_card]
    mask = (low != gone[0]) & (high != gone[0])
    for card in gone[1:]:
        mask = mask & (low != card) & (high != card)
    first = low - below(low, gone)
    second = high - below(high, gone)
    index = ((first * (2 * DECK - 1 - first)) >> 1) + second - first - 1
    chosen = jnp.where(mask, 1.0, 0.0)
    weight = jnp.concatenate([chosen[2 * t : 2 * t + 1, :HANDS] for t in range(turns)], axis=0)
    lag = jnp.where(mask & (place < HANDS), place - index, 0)
    for shift in range(SHIFTS):
        step = 1 << shift
        move = (lag >> shift) & 1
        came = pltpu.roll(move, WIDTH - step, 1)
        moves[shift] = move
        arrivals[shift] = came.astype(jnp.float32)
        lag = jnp.where(
            came == 1, pltpu.roll(lag, WIDTH - step, 1), jnp.where(move == 1, 0, lag)
        )

    copies[6].wait()
    drawn = ranks[...]
    power = jnp.exp2((drawn >> 7).astype(jnp.float32))
    mantissa = ((drawn & 127) + 128).astype(jnp.float32)
    drawn = power * mantissa
    for t in range(turns):
        wide[t, 0:rivers, :HANDS] = drawn[t * rivers : (t + 1) * rivers, :]
    both = cards[...].astype(jnp.float32)
    for t in range(turns):
        wide[turns, 8 + 2 * t : 10 + 2 * t, :] = both
    for copy in copies[7:10]:
        copy.wait()
    total = flop_reg[0]
    for a in range(1, actions):
        total = total + flop_reg[a]
    for a in range(actions):
        column = reach[0:1, :] * (flop_reg[a] / total)
        for t in range(turns):
            wide[t, 8 + a : 9 + a, :HANDS] = column
    base = reach[1:2, :]
    for a in range(actions):
        total = turn_reg[a, 0]
        for b in range(1, actions):
            total = total + turn_reg[a, b]
        mix = None
        gain = None
        for b in range(actions):
            chance = turn_reg[a, b] / total
            term = stakes[a, b] * (base * chance)
            mix = term if mix is None else mix + term
            term = stakes[a, b] * chance
            gain = term if gain is None else gain + term
        worth[a] = gain
        for t in range(turns):
            if a < 3:
                wide[t, 13 + a : 14 + a, :HANDS] = mix[t : t + 1, :]
            else:
                spot = 2 * t + a - 3
                wide[turns, spot : spot + 1, :HANDS] = mix[t : t + 1, :]

    for t in range(turns + 1):
        rows = wide[t].astype(jnp.bfloat16)
        for shift in range(SHIFTS):
            step = 1 << shift
            if t < turns:
                came = arrivals[shift, 2 * t : 2 * t + 1, :].astype(jnp.bfloat16)
                came = jnp.broadcast_to(came, rows.shape)
            else:
                came = arrivals[shift]
                came = jnp.concatenate([came, came], axis=0).astype(jnp.bfloat16)
            rows = jnp.where(came > 0.5, pltpu.roll(rows, WIDTH - step, 1), rows)
        rows = rows.astype(jnp.float32)
        if t < turns:
            keys[t * rivers : (t + 1) * rivers, :] = rows[0:8, :SPAN]
            columns[t, 0:8, :] = rows[8:16, :SPAN]
        else:
            for other in range(turns):
                columns[other, 8:10, :] = rows[2 * other : 2 * other + 2, :SPAN]
                columns[other, 10:12, :] = rows[8 + 2 * other : 10 + 2 * other, :SPAN]
    for part in range(SPAN // 128):
        lanes = slice(part * 128, (part + 1) * 128)
        keys_t[lanes, 0:boards] = keys[:, lanes].T
    copies[10].wait()
    live_count = board_count[0, 0]

    def some_boards(step, carry):
        origin = step * UNROLL
        t = origin // rivers
        held = columns[t]
        low_live = held[10:11, :].astype(jnp.int32)
        high_live = held[11:12, :].astype(jnp.int32)
        gathered = None
        for ahead in range(UNROLL):
            board = origin + ahead
            river_mask = avoid(low_live, high_live, river_cards[t, board % rivers])
            mixed = (held * river_mask).astype(jnp.bfloat16)
            row = keys[pl.ds(board, 1), :].astype(jnp.bfloat16)
            out = None
            for start in range(0, ROWS, CHUNK):
                size = min(CHUNK, ROWS - start)
                rows = slice(start, start + size)
                picked = jnp.full((size, 128), board, jnp.int32)
                column = jnp.take_along_axis(keys_t[rows, :], picked, axis=1)
                column = column.astype(jnp.bfloat16)
                column = jnp.concatenate([column] * (SPAN // 128), axis=1)
                table = jnp.clip(row - column, -1.0, 1.0) * apart[rows, :]
                part = jnp.dot(mixed[:, rows], table, preferred_element_type=jnp.float32)
                out = part if out is None else out + part
            live = jnp.where(board < live_count, 1.0, 0.0)
            out = out * (river_mask * live)
            gathered = out if gathered is None else gathered + out
        sums[t, :, :SPAN] = sums[t, :, :SPAN] + gathered
        return carry

    lax.fori_loop(0, (live_count + (UNROLL - 1)) // UNROLL, some_boards, 0)

    for t in range(turns):
        others[2 * t : 2 * t + 2, :] = sums[t, 8:10, :]
    for t in range(turns + 1):
        rows = sums[t, 0:8, :] if t < turns else others[...]
        for shift in reversed(range(SHIFTS)):
            step = 1 << shift
            move = moves[shift, 2 * t : 2 * t + 1, :] if t < turns else moves[shift]
            move = jnp.broadcast_to(move, rows.shape)
            rows = jnp.where(move == 1, pltpu.roll(rows, step, 1), rows)
        if t < turns:
            sums[t, 0:8, :] = rows
        else:
            others[...] = rows
    zero = None
    for t in range(turns):
        term = jnp.concatenate(
            [sums[t, actions:8, :HANDS], others[2 * t : 2 * t + 2, :HANDS]], axis=0
        )
        term = term * weight[t : t + 1, :]
        zero = term if zero is None else zero + term
    zero = zero / (rivers * TURNS_ALL * 1.0)
    one_share = None
    for a in range(actions):
        mean = jnp.concatenate([sums[t, a : a + 1, :HANDS] for t in range(turns)], axis=0)
        mean = mean * weight / rivers
        mean_out[a] = mean
        node = worth[a] * mean
        one_share = node if one_share is None else one_share + node
    one_share = jnp.sum(one_share, axis=0, keepdims=True) / (TURNS_ALL * 1.0)
    tiles = WIDTH // 128
    for a in range(actions + 1):
        row = zero[a : a + 1, :] if a < actions else one_share
        for part in range(tiles):
            ends = min((part + 1) * 128, HANDS)
            line = a * tiles + part
            lines[line : line + 1, 0 : ends - part * 128] = row[:, part * 128 : ends]
    for device in range(message.shape[0]):
        message[device] = lines[...]


def iterate(flop_cards, turn_cards, river_cards, board_count, stakes, reach, flop_reg, turn_reg, ranks):
    actions, _, hands = flop_reg.shape
    turns = turn_reg.shape[2]
    boards = ranks.shape[0]
    cards, apart = hand_tables()
    vmem = pl.BlockSpec(memory_space=pltpu.VMEM)
    operands = (
        flop_cards,
        turn_cards,
        river_cards,
        board_count,
        stakes,
        jnp.asarray(cards),
        ranks,
        reach,
        flop_reg,
        turn_reg,
        jnp.asarray(apart.astype(jnp.bfloat16)),
    )
    return pl.pallas_call(
        iteration_kernel,
        out_shape=(
            jax.ShapeDtypeStruct((actions, turns, hands), jnp.float32),
            jax.ShapeDtypeStruct((DEVICES, LINES, 128), jnp.float32),
        ),
        in_specs=[pl.BlockSpec(memory_space=pltpu.HBM)] * len(operands),
        out_specs=(vmem, vmem),
        scratch_shapes=[pltpu.SMEM(held.shape, held.dtype) for held in operands[:5]]
        + [pltpu.VMEM(held.shape, held.dtype) for held in operands[5:]]
        + [
            pltpu.VMEM((turns + 1, 16, WIDTH), jnp.float32),
            pltpu.VMEM((SHIFTS, 2 * turns, WIDTH), jnp.int32),
            pltpu.VMEM((SHIFTS, 2 * turns, WIDTH), jnp.float32),
            pltpu.VMEM((boards, SPAN), jnp.float32),
            pltpu.VMEM((SPAN, 128), jnp.float32),
            pltpu.VMEM((turns, 16, SPAN), jnp.float32),
            pltpu.VMEM((actions, turns, hands), jnp.float32),
            pltpu.VMEM((turns, 16, WIDTH), jnp.float32),
            pltpu.VMEM((2 * turns, WIDTH), jnp.float32),
            pltpu.VMEM((LINES, 128), jnp.float32),
            pltpu.SemaphoreType.DMA((len(operands),)),
        ],
        compiler_params=pltpu.CompilerParams(vmem_limit_bytes=62 * 1024 * 1024),
        cost_estimate=pl.CostEstimate(
            flops=32 * 2 * 16 * HANDS * HANDS, bytes_accessed=5000000, transcendentals=0
        ),
        name="iteration",
    )(*operands)


def regret_kernel(stakes, mean, turn_reg, turn_next):
    actions = turn_reg.shape[0]
    for a in range(actions):
        total = turn_reg[a, 0]
        for b in range(1, actions):
            total = total + turn_reg[a, b]
        values = [stakes[a, b] * mean[a] for b in range(actions)]
        node = None
        for b in range(actions):
            term = (turn_reg[a, b] / total) * values[b]
            node = term if node is None else node + term
        for b in range(actions):
            turn_next[a, b] = jnp.maximum(turn_reg[a, b] + values[b] - node, 0.0)


def updated(stakes, mean, turn_reg):
    vmem = pl.BlockSpec(memory_space=pltpu.VMEM)
    return pl.pallas_call(
        regret_kernel,
        out_shape=jax.ShapeDtypeStruct(turn_reg.shape, jnp.float32),
        in_specs=[pl.BlockSpec(memory_space=pltpu.SMEM), vmem, vmem],
        out_specs=vmem,
        cost_estimate=pl.CostEstimate(flops=2000000, bytes_accessed=1200000, transcendentals=0),
        name="turn_regrets",
    )(stakes, mean, turn_reg)


def summed(block, axis, groups=None):
    count = lax.axis_size(axis) if groups is None else len(groups[0])
    spread = jnp.broadcast_to(block[None], (count,) + block.shape)
    heard = lax.all_to_all(spread, axis, 0, 0, axis_index_groups=groups, tiled=True)
    return jnp.sum(heard, axis=0)


def tiled(rows):
    count = rows.size
    padded = -(-count // 1024) * 1024
    return jnp.pad(rows.reshape(-1), (0, padded - count)).reshape(-1, 128)


def per_device(
    root_reach,
    stakes,
    flop_regrets,
    turn_regrets,
    flop_cards,
    turn_cards,
    river_cards,
    hand_ranks,
    board_count,
):
    actions = flop_regrets.shape[1]
    hands = flop_regrets.shape[2]
    turns = turn_cards.shape[1]
    rivers = river_cards.shape[2]
    flop_reg = jnp.transpose(flop_regrets, (1, 0, 2))
    turn_reg = jnp.transpose(turn_regrets[0], (0, 2, 1, 3))
    mean, message = iterate(
        flop_cards,
        turn_cards,
        river_cards[0],
        board_count,
        stakes,
        root_reach,
        flop_reg,
        turn_reg,
        hand_ranks.reshape(turns * rivers, hands),
    )
    heard = lax.all_to_all(message, "turn", 0, 0, tiled=True)
    heard = jnp.sum(heard, axis=0)[: (actions + 1) * (WIDTH // 128)]
    total = heard.reshape(actions + 1, WIDTH)[:, :hands]
    regrets = flop_regrets[0]
    flop_policy = regrets / jnp.sum(regrets, axis=0, keepdims=True)
    zero_flop = jnp.sum(flop_policy * total[:actions], axis=0)
    values = tiled(jnp.stack([zero_flop, total[actions]]))
    flops = lax.axis_size("flop")
    near = [list(range(i, i + 4)) for i in range(0, flops, 4)]
    far = [list(range(i, flops, 4)) for i in range(4)]
    values = summed(values, "flop", near)
    values, total, zero_flop, mean = lax.optimization_barrier((values, total, zero_flop, mean))
    turn_new = updated(stakes, mean, turn_reg)
    turn_next = jnp.transpose(turn_new, (0, 2, 1, 3))[None]
    flop_next = jnp.maximum(regrets + total[:actions] - zero_flop, 0.0)[None]
    values = summed(values, "flop", far)
    root_values = values.reshape(-1)[: 2 * hands].reshape(2, hands)
    return (flop_next, turn_next, root_values)


def solution(mesh):
    in_specs = (
        P(),
        P(),
        P("flop", None, None),
        P("flop", None, "turn", None, None),
        P("flop", None),
        P("flop", "turn"),
        P("flop", "turn", None),
        P("flop", "turn", None, None),
        P("flop", "turn"),
    )
    out_specs = (P("flop", None, None), P("flop", None, "turn", None, None), P())
    return jax.shard_map(
        per_device, mesh=mesh, in_specs=in_specs, out_specs=out_specs, check_vma=False
    )
```

```python
import jax
import jax.numpy as jnp
import numpy as np
from jax import lax
from jax.experimental import pallas as pl
from jax.experimental.pallas import tpu as pltpu
from jax.sharding import PartitionSpec as P

HANDS = 1326
WIDTH = 1408
DECK = 48
LIVE = 1128
ROWS = 1136
SPAN = 1152
SHIFTS = 8
CHUNK = 256
UNROLL = 16
TURNS_ALL = 32
DEVICES = 8


def hand_tables():
    low, high = np.triu_indices(52, 1)
    cards = np.full((2, WIDTH), 99, np.int32)
    cards[0, :HANDS] = low
    cards[1, :HANDS] = high
    low, high = np.triu_indices(DECK, 1)
    share = (low[:, None] == low[None, :]) | (low[:, None] == high[None, :])
    share |= (high[:, None] == low[None, :]) | (high[:, None] == high[None, :])
    apart = np.zeros((ROWS, SPAN), np.float32)
    apart[:LIVE, :LIVE] = ~share
    return cards, apart


def avoid(low, high, card):
    return jnp.where((low != card) & (high != card), 1.0, 0.0)


def below(card, cards):
    count = (card > cards[0]).astype(jnp.int32)
    for other in cards[1:]:
        count = count + (card > other).astype(jnp.int32)
    return count


def iteration_kernel(
    flop_cards_hbm,
    turn_cards_hbm,
    river_cards_hbm,
    board_count_hbm,
    stakes_hbm,
    cards_hbm,
    ranks_hbm,
    reach_hbm,
    flop_reg_hbm,
    turn_reg_hbm,
    apart_hbm,
    mean_out,
    message,
    flop_cards,
    turn_cards,
    river_cards,
    board_count,
    stakes,
    cards,
    ranks,
    reach,
    flop_reg,
    turn_reg,
    apart,
    wide,
    moves,
    arrivals,
    keys,
    keys_t,
    columns,
    worth,
    sums,
    others,
    arrived,
):
    actions = flop_reg.shape[0]
    turns = turn_reg.shape[2]
    boards = ranks.shape[0]
    rivers = boards // turns
    pairs = (
        (flop_cards_hbm, flop_cards),
        (turn_cards_hbm, turn_cards),
        (river_cards_hbm, river_cards),
        (board_count_hbm, board_count),
        (stakes_hbm, stakes),
        (cards_hbm, cards),
        (ranks_hbm, ranks),
        (reach_hbm, reach),
        (flop_reg_hbm, flop_reg),
        (turn_reg_hbm, turn_reg),
        (apart_hbm, apart),
    )
    copies = [
        pltpu.make_async_copy(source, held, arrived.at[spot])
        for spot, (source, held) in enumerate(pairs)
    ]
    for copy in copies:
        copy.start()

    tail = slice(WIDTH - 128, WIDTH)
    wide[:, :, tail] = jnp.zeros((turns + 1, 16, 128), jnp.float32)
    sums[...] = jnp.zeros(sums.shape, jnp.float32)
    for t in range(turns):
        columns[t, 8:16, :] = jnp.zeros((8, SPAN), jnp.float32)
    for copy in copies[:6]:
        copy.wait()

    shape = (2 * turns, WIDTH)
    low = jnp.broadcast_to(cards[0:1, :], shape)
    high = jnp.broadcast_to(cards[1:2, :], shape)
    place = lax.broadcasted_iota(jnp.int32, shape, 1)
    which = lax.broadcasted_iota(jnp.int32, shape, 0) >> 1
    turn_card = jnp.full(shape, turn_cards[0, 0], jnp.int32)
    for t in range(1, turns):
        turn_card = jnp.where(which == t, turn_cards[0, t], turn_card)
    gone = [flop_cards[0, 0], flop_cards[0, 1], flop_cards[0, 2], turn_card]
    mask = (low != gone[0]) & (high != gone[0])
    for card in gone[1:]:
        mask = mask & (low != card) & (high != card)
    first = low - below(low, gone)
    second = high - below(high, gone)
    index = ((first * (2 * DECK - 1 - first)) >> 1) + second - first - 1
    chosen = jnp.where(mask, 1.0, 0.0)
    weight = jnp.concatenate([chosen[2 * t : 2 * t + 1, :HANDS] for t in range(turns)], axis=0)
    lag = jnp.where(mask & (place < HANDS), place - index, 0)
    for shift in range(SHIFTS):
        step = 1 << shift
        move = (lag >> shift) & 1
        came = pltpu.roll(move, WIDTH - step, 1)
        moves[shift] = move
        arrivals[shift] = came.astype(jnp.float32)
        lag = jnp.where(
            came == 1, pltpu.roll(lag, WIDTH - step, 1), jnp.where(move == 1, 0, lag)
        )

    copies[6].wait()
    drawn = ranks[...]
    power = jnp.exp2((drawn >> 7).astype(jnp.float32))
    mantissa = ((drawn & 127) + 128).astype(jnp.float32)
    drawn = power * mantissa
    for t in range(turns):
        wide[t, 0:rivers, :HANDS] = drawn[t * rivers : (t + 1) * rivers, :]
    both = cards[...].astype(jnp.float32)
    for t in range(turns):
        wide[turns, 8 + 2 * t : 10 + 2 * t, :] = both
    for copy in copies[7:10]:
        copy.wait()
    total = flop_reg[0]
    for a in range(1, actions):
        total = total + flop_reg[a]
    for a in range(actions):
        column = reach[0:1, :] * (flop_reg[a] / total)
        for t in range(turns):
            wide[t, 8 + a : 9 + a, :HANDS] = column
    base = reach[1:2, :]
    for a in range(actions):
        total = turn_reg[a, 0]
        for b in range(1, actions):
            total = total + turn_reg[a, b]
        mix = None
        gain = None
        for b in range(actions):
            chance = turn_reg[a, b] / total
            term = stakes[a, b] * (base * chance)
            mix = term if mix is None else mix + term
            term = stakes[a, b] * chance
            gain = term if gain is None else gain + term
        worth[a] = gain
        for t in range(turns):
            if a < 3:
                wide[t, 13 + a : 14 + a, :HANDS] = mix[t : t + 1, :]
            else:
                spot = 2 * t + a - 3
                wide[turns, spot : spot + 1, :HANDS] = mix[t : t + 1, :]

    for t in range(turns + 1):
        rows = wide[t].astype(jnp.bfloat16)
        for shift in range(SHIFTS):
            step = 1 << shift
            if t < turns:
                came = arrivals[shift, 2 * t : 2 * t + 1, :].astype(jnp.bfloat16)
                came = jnp.broadcast_to(came, rows.shape)
            else:
                came = arrivals[shift]
                came = jnp.concatenate([came, came], axis=0).astype(jnp.bfloat16)
            rows = jnp.where(came > 0.5, pltpu.roll(rows, WIDTH - step, 1), rows)
        rows = rows.astype(jnp.float32)
        if t < turns:
            keys[t * rivers : (t + 1) * rivers, :] = rows[0:8, :SPAN]
            columns[t, 0:8, :] = rows[8:16, :SPAN]
        else:
            for other in range(turns):
                columns[other, 8:10, :] = rows[2 * other : 2 * other + 2, :SPAN]
                columns[other, 10:12, :] = rows[8 + 2 * other : 10 + 2 * other, :SPAN]
    for part in range(SPAN // 128):
        lanes = slice(part * 128, (part + 1) * 128)
        keys_t[lanes, 0:boards] = keys[:, lanes].T
    copies[10].wait()
    live_count = board_count[0, 0]

    def some_boards(step, carry):
      for part in range(UNROLL // rivers):
        origin = step * UNROLL + part * rivers
        t = step * (UNROLL // rivers) + part
        held = columns[t]
        low_live = held[10:11, :].astype(jnp.int32)
        high_live = held[11:12, :].astype(jnp.int32)
        gathered = None
        for ahead in range(rivers):
            board = origin + ahead
            river_mask = avoid(low_live, high_live, river_cards[t, board % rivers])
            mixed = (held * river_mask).astype(jnp.bfloat16)
            row = keys[pl.ds(board, 1), :].astype(jnp.bfloat16)
            out = None
            for start in range(0, ROWS, CHUNK):
                size = min(CHUNK, ROWS - start)
                rows = slice(start, start + size)
                picked = jnp.full((size, 128), board, jnp.int32)
                column = jnp.take_along_axis(keys_t[rows, :], picked, axis=1)
                column = column.astype(jnp.bfloat16)
                column = jnp.concatenate([column] * (SPAN // 128), axis=1)
                table = jnp.clip(row - column, -1.0, 1.0) * apart[rows, :]
                part = jnp.dot(mixed[:, rows], table, preferred_element_type=jnp.float32)
                out = part if out is None else out + part
            live = jnp.where(board < live_count, 1.0, 0.0)
            out = out * (river_mask * live)
            gathered = out if gathered is None else gathered + out
        sums[t, :, :SPAN] = sums[t, :, :SPAN] + gathered
      return carry

    lax.fori_loop(0, (live_count + (UNROLL - 1)) // UNROLL, some_boards, 0)

    for t in range(turns):
        others[2 * t : 2 * t + 2, :] = sums[t, 8:10, :]
    for t in range(turns + 1):
        rows = sums[t, 0:8, :] if t < turns else others[...]
        for shift in reversed(range(SHIFTS)):
            step = 1 << shift
            move = moves[shift, 2 * t : 2 * t + 1, :] if t < turns else moves[shift]
            move = jnp.broadcast_to(move, rows.shape)
            rows = jnp.where(move == 1, pltpu.roll(rows, step, 1), rows)
        if t < turns:
            sums[t, 0:8, :] = rows
        else:
            others[...] = rows
    zero = None
    for t in range(turns):
        term = jnp.concatenate(
            [sums[t, actions:8, :HANDS], others[2 * t : 2 * t + 2, :HANDS]], axis=0
        )
        term = term * weight[t : t + 1, :]
        zero = term if zero is None else zero + term
    zero = zero / (rivers * TURNS_ALL * 1.0)
    one_share = None
    for a in range(actions):
        mean = jnp.concatenate([sums[t, a : a + 1, :HANDS] for t in range(turns)], axis=0)
        mean = mean * weight / rivers
        mean_out[a] = mean
        node = worth[a] * mean
        one_share = node if one_share is None else one_share + node
    one_share = jnp.sum(one_share, axis=0, keepdims=True) / (TURNS_ALL * 1.0)
    rows = jnp.concatenate([zero, one_share], axis=0)
    for device in range(message.shape[0]):
        for pair in range((actions + 1) // 2):
            message[device, pair] = rows[2 * pair : 2 * pair + 2, :]


def iterate(flop_cards, turn_cards, river_cards, board_count, stakes, reach, flop_reg, turn_reg, ranks):
    actions, _, hands = flop_reg.shape
    turns = turn_reg.shape[2]
    boards = ranks.shape[0]
    cards, apart = hand_tables()
    vmem = pl.BlockSpec(memory_space=pltpu.VMEM)
    operands = (
        flop_cards,
        turn_cards,
        river_cards,
        board_count,
        stakes,
        jnp.asarray(cards),
        ranks,
        reach,
        flop_reg,
        turn_reg,
        jnp.asarray(apart.astype(jnp.bfloat16)),
    )
    return pl.pallas_call(
        iteration_kernel,
        out_shape=(
            jax.ShapeDtypeStruct((actions, turns, hands), jnp.float32),
            jax.ShapeDtypeStruct((DEVICES, (actions + 1) // 2, 2, hands), jnp.float32),
        ),
        in_specs=[pl.BlockSpec(memory_space=pltpu.HBM)] * len(operands),
        out_specs=(vmem, vmem),
        scratch_shapes=[pltpu.SMEM(held.shape, held.dtype) for held in operands[:5]]
        + [pltpu.VMEM(held.shape, held.dtype) for held in operands[5:]]
        + [
            pltpu.VMEM((turns + 1, 16, WIDTH), jnp.float32),
            pltpu.VMEM((SHIFTS, 2 * turns, WIDTH), jnp.int32),
            pltpu.VMEM((SHIFTS, 2 * turns, WIDTH), jnp.float32),
            pltpu.VMEM((boards, SPAN), jnp.float32),
            pltpu.VMEM((SPAN, 128), jnp.float32),
            pltpu.VMEM((turns, 16, SPAN), jnp.float32),
            pltpu.VMEM((actions, turns, hands), jnp.float32),
            pltpu.VMEM((turns, 16, WIDTH), jnp.float32),
            pltpu.VMEM((2 * turns, WIDTH), jnp.float32),
            pltpu.SemaphoreType.DMA((len(operands),)),
        ],
        compiler_params=pltpu.CompilerParams(vmem_limit_bytes=62 * 1024 * 1024),
        cost_estimate=pl.CostEstimate(
            flops=32 * 2 * 16 * HANDS * HANDS, bytes_accessed=5000000, transcendentals=0
        ),
        name="iteration",
    )(*operands)


def regret_kernel(stakes, mean, turn_reg, turn_next):
    actions = turn_reg.shape[0]
    for a in range(actions):
        total = turn_reg[a, 0]
        for b in range(1, actions):
            total = total + turn_reg[a, b]
        values = [stakes[a, b] * mean[a] for b in range(actions)]
        node = None
        for b in range(actions):
            term = (turn_reg[a, b] / total) * values[b]
            node = term if node is None else node + term
        for b in range(actions):
            turn_next[a, b] = jnp.maximum(turn_reg[a, b] + values[b] - node, 0.0)


def updated(stakes, mean, turn_reg):
    vmem = pl.BlockSpec(memory_space=pltpu.VMEM)
    return pl.pallas_call(
        regret_kernel,
        out_shape=jax.ShapeDtypeStruct(turn_reg.shape, jnp.float32),
        in_specs=[pl.BlockSpec(memory_space=pltpu.SMEM), vmem, vmem],
        out_specs=vmem,
        cost_estimate=pl.CostEstimate(flops=2000000, bytes_accessed=1200000, transcendentals=0),
        name="turn_regrets",
    )(stakes, mean, turn_reg)


def summed(block, axis, groups=None):
    count = lax.axis_size(axis) if groups is None else len(groups[0])
    spread = jnp.broadcast_to(block[None], (count,) + block.shape)
    heard = lax.all_to_all(spread, axis, 0, 0, axis_index_groups=groups, tiled=True)
    return jnp.sum(heard, axis=0)


def per_device(
    root_reach,
    stakes,
    flop_regrets,
    turn_regrets,
    flop_cards,
    turn_cards,
    river_cards,
    hand_ranks,
    board_count,
):
    actions = flop_regrets.shape[1]
    hands = flop_regrets.shape[2]
    turns = turn_cards.shape[1]
    rivers = river_cards.shape[2]
    flop_reg = jnp.transpose(flop_regrets, (1, 0, 2))
    turn_reg = jnp.transpose(turn_regrets[0], (0, 2, 1, 3))
    mean, message = iterate(
        flop_cards,
        turn_cards,
        river_cards[0],
        board_count,
        stakes,
        root_reach,
        flop_reg,
        turn_reg,
        hand_ranks.reshape(turns * rivers, hands),
    )
    heard = lax.all_to_all(message, "turn", 0, 0, tiled=True)
    total = jnp.sum(heard, axis=0).reshape(actions + 1, hands)
    regrets = flop_regrets[0]
    flop_policy = regrets / jnp.sum(regrets, axis=0, keepdims=True)
    zero_flop = jnp.sum(flop_policy * total[:actions], axis=0)
    values = jnp.stack([zero_flop, total[actions]])
    flops = lax.axis_size("flop")
    near = [list(range(i, i + 4)) for i in range(0, flops, 4)]
    far = [list(range(i, flops, 4)) for i in range(4)]
    values = summed(values, "flop", near)
    values, total, zero_flop, mean = lax.optimization_barrier((values, total, zero_flop, mean))
    turn_new = updated(stakes, mean, turn_reg)
    turn_next = jnp.transpose(turn_new, (0, 2, 1, 3))[None]
    flop_next = jnp.maximum(regrets + total[:actions] - zero_flop, 0.0)[None]
    values = summed(values, "flop", far)
    return (flop_next, turn_next, values)


def solution(mesh):
    in_specs = (
        P(),
        P(),
        P("flop", None, None),
        P("flop", None, "turn", None, None),
        P("flop", None),
        P("flop", "turn"),
        P("flop", "turn", None),
        P("flop", "turn", None, None),
        P("flop", "turn"),
    )
    out_specs = (P("flop", None, None), P("flop", None, "turn", None, None), P())
    return jax.shard_map(
        per_device, mesh=mesh, in_specs=in_specs, out_specs=out_specs, check_vma=False
    )
```

```python
import jax
import jax.numpy as jnp
import numpy as np
from jax import lax
from jax.experimental import pallas as pl
from jax.experimental.pallas import tpu as pltpu
from jax.sharding import PartitionSpec as P

HANDS = 1326
WIDTH = 1408
DECK = 48
LIVE = 1128
ROWS = 1136
SPAN = 1152
SHIFTS = 8
CHUNK = 256
UNROLL = 32
TURNS_ALL = 32
DEVICES = 8


def hand_tables():
    low, high = np.triu_indices(52, 1)
    cards = np.full((2, WIDTH), 99, np.int32)
    cards[0, :HANDS] = low
    cards[1, :HANDS] = high
    low, high = np.triu_indices(DECK, 1)
    share = (low[:, None] == low[None, :]) | (low[:, None] == high[None, :])
    share |= (high[:, None] == low[None, :]) | (high[:, None] == high[None, :])
    apart = np.zeros((ROWS, SPAN), np.float32)
    apart[:LIVE, :LIVE] = ~share
    return cards, apart


def avoid(low, high, card):
    return jnp.where((low != card) & (high != card), 1.0, 0.0)


def below(card, cards):
    count = (card > cards[0]).astype(jnp.int32)
    for other in cards[1:]:
        count = count + (card > other).astype(jnp.int32)
    return count


def iteration_kernel(
    flop_cards_hbm,
    turn_cards_hbm,
    river_cards_hbm,
    board_count_hbm,
    stakes_hbm,
    cards_hbm,
    ranks_hbm,
    reach_hbm,
    flop_reg_hbm,
    turn_reg_hbm,
    apart_hbm,
    mean_out,
    message,
    flop_cards,
    turn_cards,
    river_cards,
    board_count,
    stakes,
    cards,
    ranks,
    reach,
    flop_reg,
    turn_reg,
    apart,
    wide,
    moves,
    arrivals,
    keys,
    keys_t,
    columns,
    worth,
    sums,
    others,
    arrived,
):
    actions = flop_reg.shape[0]
    turns = turn_reg.shape[2]
    boards = ranks.shape[0]
    rivers = boards // turns
    pairs = (
        (flop_cards_hbm, flop_cards),
        (turn_cards_hbm, turn_cards),
        (river_cards_hbm, river_cards),
        (board_count_hbm, board_count),
        (stakes_hbm, stakes),
        (cards_hbm, cards),
        (ranks_hbm, ranks),
        (reach_hbm, reach),
        (flop_reg_hbm, flop_reg),
        (turn_reg_hbm, turn_reg),
        (apart_hbm, apart),
    )
    copies = [
        pltpu.make_async_copy(source, held, arrived.at[spot])
        for spot, (source, held) in enumerate(pairs)
    ]
    for copy in copies:
        copy.start()

    tail = slice(WIDTH - 128, WIDTH)
    wide[:, :, tail] = jnp.zeros((turns + 1, 16, 128), jnp.float32)
    sums[...] = jnp.zeros(sums.shape, jnp.float32)
    for t in range(turns):
        columns[t, 8:16, :] = jnp.zeros((8, SPAN), jnp.float32)
    for copy in copies[:6]:
        copy.wait()

    shape = (2 * turns, WIDTH)
    low = jnp.broadcast_to(cards[0:1, :], shape)
    high = jnp.broadcast_to(cards[1:2, :], shape)
    place = lax.broadcasted_iota(jnp.int32, shape, 1)
    which = lax.broadcasted_iota(jnp.int32, shape, 0) >> 1
    turn_card = jnp.full(shape, turn_cards[0, 0], jnp.int32)
    for t in range(1, turns):
        turn_card = jnp.where(which == t, turn_cards[0, t], turn_card)
    gone = [flop_cards[0, 0], flop_cards[0, 1], flop_cards[0, 2], turn_card]
    mask = (low != gone[0]) & (high != gone[0])
    for card in gone[1:]:
        mask = mask & (low != card) & (high != card)
    first = low - below(low, gone)
    second = high - below(high, gone)
    index = ((first * (2 * DECK - 1 - first)) >> 1) + second - first - 1
    chosen = jnp.where(mask, 1.0, 0.0)
    weight = jnp.concatenate([chosen[2 * t : 2 * t + 1, :HANDS] for t in range(turns)], axis=0)
    lag = jnp.where(mask & (place < HANDS), place - index, 0)
    for shift in range(SHIFTS):
        step = 1 << shift
        move = (lag >> shift) & 1
        came = pltpu.roll(move, WIDTH - step, 1)
        moves[shift] = move
        arrivals[shift] = came.astype(jnp.float32)
        lag = jnp.where(
            came == 1, pltpu.roll(lag, WIDTH - step, 1), jnp.where(move == 1, 0, lag)
        )

    copies[6].wait()
    drawn = ranks[...]
    power = jnp.exp2((drawn >> 7).astype(jnp.float32))
    mantissa = ((drawn & 127) + 128).astype(jnp.float32)
    drawn = power * mantissa
    for t in range(turns):
        wide[t, 0:rivers, :HANDS] = drawn[t * rivers : (t + 1) * rivers, :]
    both = cards[...].astype(jnp.float32)
    for t in range(turns):
        wide[turns, 8 + 2 * t : 10 + 2 * t, :] = both
    for copy in copies[7:10]:
        copy.wait()
    total = flop_reg[0]
    for a in range(1, actions):
        total = total + flop_reg[a]
    for a in range(actions):
        column = reach[0:1, :] * (flop_reg[a] / total)
        for t in range(turns):
            wide[t, 8 + a : 9 + a, :HANDS] = column
    base = reach[1:2, :]
    for a in range(actions):
        total = turn_reg[a, 0]
        for b in range(1, actions):
            total = total + turn_reg[a, b]
        mix = None
        gain = None
        for b in range(actions):
            chance = turn_reg[a, b] / total
            term = stakes[a, b] * (base * chance)
            mix = term if mix is None else mix + term
            term = stakes[a, b] * chance
            gain = term if gain is None else gain + term
        worth[a] = gain
        for t in range(turns):
            if a < 3:
                wide[t, 13 + a : 14 + a, :HANDS] = mix[t : t + 1, :]
            else:
                spot = 2 * t + a - 3
                wide[turns, spot : spot + 1, :HANDS] = mix[t : t + 1, :]

    for t in range(turns + 1):
        rows = wide[t].astype(jnp.bfloat16)
        for shift in range(SHIFTS):
            step = 1 << shift
            if t < turns:
                came = arrivals[shift, 2 * t : 2 * t + 1, :].astype(jnp.bfloat16)
                came = jnp.broadcast_to(came, rows.shape)
            else:
                came = arrivals[shift]
                came = jnp.concatenate([came, came], axis=0).astype(jnp.bfloat16)
            rows = jnp.where(came > 0.5, pltpu.roll(rows, WIDTH - step, 1), rows)
        rows = rows.astype(jnp.float32)
        if t < turns:
            keys[t * rivers : (t + 1) * rivers, :] = rows[0:8, :SPAN]
            columns[t, 0:8, :] = rows[8:16, :SPAN]
        else:
            for other in range(turns):
                columns[other, 8:10, :] = rows[2 * other : 2 * other + 2, :SPAN]
                columns[other, 10:12, :] = rows[8 + 2 * other : 10 + 2 * other, :SPAN]
    for part in range(SPAN // 128):
        lanes = slice(part * 128, (part + 1) * 128)
        keys_t[lanes, 0:boards] = keys[:, lanes].T
    copies[10].wait()
    live_count = board_count[0, 0]

    def some_boards(step, carry):
      for part in range(UNROLL // rivers):
        origin = step * UNROLL + part * rivers
        t = step * (UNROLL // rivers) + part
        held = columns[t]
        low_live = held[10:11, :].astype(jnp.int32)
        high_live = held[11:12, :].astype(jnp.int32)
        gathered = None
        for ahead in range(rivers):
            board = origin + ahead
            river_mask = avoid(low_live, high_live, river_cards[t, board % rivers])
            mixed = (held * river_mask).astype(jnp.bfloat16)
            row = keys[pl.ds(board, 1), :].astype(jnp.bfloat16)
            out = None
            for start in range(0, ROWS, CHUNK):
                size = min(CHUNK, ROWS - start)
                rows = slice(start, start + size)
                picked = jnp.full((size, 128), board, jnp.int32)
                column = jnp.take_along_axis(keys_t[rows, :], picked, axis=1)
                column = column.astype(jnp.bfloat16)
                column = jnp.concatenate([column] * (SPAN // 128), axis=1)
                table = jnp.clip(row - column, -1.0, 1.0) * apart[rows, :]
                part = jnp.dot(mixed[:, rows], table, preferred_element_type=jnp.float32)
                out = part if out is None else out + part
            live = jnp.where(board < live_count, 1.0, 0.0)
            out = out * (river_mask * live)
            gathered = out if gathered is None else gathered + out
        sums[t, :, :SPAN] = sums[t, :, :SPAN] + gathered
      return carry

    lax.fori_loop(0, (live_count + (UNROLL - 1)) // UNROLL, some_boards, 0)

    for t in range(turns):
        others[2 * t : 2 * t + 2, :] = sums[t, 8:10, :]
    for t in range(turns + 1):
        rows = sums[t, 0:8, :] if t < turns else others[...]
        for shift in reversed(range(SHIFTS)):
            step = 1 << shift
            move = moves[shift, 2 * t : 2 * t + 1, :] if t < turns else moves[shift]
            move = jnp.broadcast_to(move, rows.shape)
            rows = jnp.where(move == 1, pltpu.roll(rows, step, 1), rows)
        if t < turns:
            sums[t, 0:8, :] = rows
        else:
            others[...] = rows
    zero = None
    for t in range(turns):
        term = jnp.concatenate(
            [sums[t, actions:8, :HANDS], others[2 * t : 2 * t + 2, :HANDS]], axis=0
        )
        term = term * weight[t : t + 1, :]
        zero = term if zero is None else zero + term
    zero = zero / (rivers * TURNS_ALL * 1.0)
    one_share = None
    for a in range(actions):
        mean = jnp.concatenate([sums[t, a : a + 1, :HANDS] for t in range(turns)], axis=0)
        mean = mean * weight / rivers
        mean_out[a] = mean
        node = worth[a] * mean
        one_share = node if one_share is None else one_share + node
    one_share = jnp.sum(one_share, axis=0, keepdims=True) / (TURNS_ALL * 1.0)
    rows = jnp.concatenate([zero, one_share], axis=0)
    for device in range(message.shape[0]):
        for pair in range((actions + 1) // 2):
            message[device, pair] = rows[2 * pair : 2 * pair + 2, :]


def iterate(flop_cards, turn_cards, river_cards, board_count, stakes, reach, flop_reg, turn_reg, ranks):
    actions, _, hands = flop_reg.shape
    turns = turn_reg.shape[2]
    boards = ranks.shape[0]
    cards, apart = hand_tables()
    vmem = pl.BlockSpec(memory_space=pltpu.VMEM)
    operands = (
        flop_cards,
        turn_cards,
        river_cards,
        board_count,
        stakes,
        jnp.asarray(cards),
        ranks,
        reach,
        flop_reg,
        turn_reg,
        jnp.asarray(apart.astype(jnp.bfloat16)),
    )
    return pl.pallas_call(
        iteration_kernel,
        out_shape=(
            jax.ShapeDtypeStruct((actions, turns, hands), jnp.float32),
            jax.ShapeDtypeStruct((DEVICES, (actions + 1) // 2, 2, hands), jnp.float32),
        ),
        in_specs=[pl.BlockSpec(memory_space=pltpu.HBM)] * len(operands),
        out_specs=(vmem, vmem),
        scratch_shapes=[pltpu.SMEM(held.shape, held.dtype) for held in operands[:5]]
        + [pltpu.VMEM(held.shape, held.dtype) for held in operands[5:]]
        + [
            pltpu.VMEM((turns + 1, 16, WIDTH), jnp.float32),
            pltpu.VMEM((SHIFTS, 2 * turns, WIDTH), jnp.int32),
            pltpu.VMEM((SHIFTS, 2 * turns, WIDTH), jnp.float32),
            pltpu.VMEM((boards, SPAN), jnp.float32),
            pltpu.VMEM((SPAN, 128), jnp.float32),
            pltpu.VMEM((turns, 16, SPAN), jnp.float32),
            pltpu.VMEM((actions, turns, hands), jnp.float32),
            pltpu.VMEM((turns, 16, WIDTH), jnp.float32),
            pltpu.VMEM((2 * turns, WIDTH), jnp.float32),
            pltpu.SemaphoreType.DMA((len(operands),)),
        ],
        compiler_params=pltpu.CompilerParams(vmem_limit_bytes=62 * 1024 * 1024),
        cost_estimate=pl.CostEstimate(
            flops=32 * 2 * 16 * HANDS * HANDS, bytes_accessed=5000000, transcendentals=0
        ),
        name="iteration",
    )(*operands)


def regret_kernel(stakes, mean, turn_reg, turn_next):
    actions = turn_reg.shape[0]
    for a in range(actions):
        total = turn_reg[a, 0]
        for b in range(1, actions):
            total = total + turn_reg[a, b]
        values = [stakes[a, b] * mean[a] for b in range(actions)]
        node = None
        for b in range(actions):
            term = (turn_reg[a, b] / total) * values[b]
            node = term if node is None else node + term
        for b in range(actions):
            turn_next[a, b] = jnp.maximum(turn_reg[a, b] + values[b] - node, 0.0)


def updated(stakes, mean, turn_reg):
    vmem = pl.BlockSpec(memory_space=pltpu.VMEM)
    return pl.pallas_call(
        regret_kernel,
        out_shape=jax.ShapeDtypeStruct(turn_reg.shape, jnp.float32),
        in_specs=[pl.BlockSpec(memory_space=pltpu.SMEM), vmem, vmem],
        out_specs=vmem,
        cost_estimate=pl.CostEstimate(flops=2000000, bytes_accessed=1200000, transcendentals=0),
        name="turn_regrets",
    )(stakes, mean, turn_reg)


def summed(block, axis, groups=None):
    count = lax.axis_size(axis) if groups is None else len(groups[0])
    spread = jnp.broadcast_to(block[None], (count,) + block.shape)
    heard = lax.all_to_all(spread, axis, 0, 0, axis_index_groups=groups, tiled=True)
    return jnp.sum(heard, axis=0)


def per_device(
    root_reach,
    stakes,
    flop_regrets,
    turn_regrets,
    flop_cards,
    turn_cards,
    river_cards,
    hand_ranks,
    board_count,
):
    actions = flop_regrets.shape[1]
    hands = flop_regrets.shape[2]
    turns = turn_cards.shape[1]
    rivers = river_cards.shape[2]
    flop_reg = jnp.transpose(flop_regrets, (1, 0, 2))
    turn_reg = jnp.transpose(turn_regrets[0], (0, 2, 1, 3))
    mean, message = iterate(
        flop_cards,
        turn_cards,
        river_cards[0],
        board_count,
        stakes,
        root_reach,
        flop_reg,
        turn_reg,
        hand_ranks.reshape(turns * rivers, hands),
    )
    heard = lax.all_to_all(message, "turn", 0, 0, tiled=True)
    total = jnp.sum(heard, axis=0).reshape(actions + 1, hands)
    regrets = flop_regrets[0]
    flop_policy = regrets / jnp.sum(regrets, axis=0, keepdims=True)
    zero_flop = jnp.sum(flop_policy * total[:actions], axis=0)
    values = jnp.stack([zero_flop, total[actions]])
    flops = lax.axis_size("flop")
    near = [list(range(i, i + 4)) for i in range(0, flops, 4)]
    far = [list(range(i, flops, 4)) for i in range(4)]
    values = summed(values, "flop", near)
    values, total, zero_flop, mean = lax.optimization_barrier((values, total, zero_flop, mean))
    turn_new = updated(stakes, mean, turn_reg)
    turn_next = jnp.transpose(turn_new, (0, 2, 1, 3))[None]
    flop_next = jnp.maximum(regrets + total[:actions] - zero_flop, 0.0)[None]
    values = summed(values, "flop", far)
    return (flop_next, turn_next, values)


def solution(mesh):
    in_specs = (
        P(),
        P(),
        P("flop", None, None),
        P("flop", None, "turn", None, None),
        P("flop", None),
        P("flop", "turn"),
        P("flop", "turn", None),
        P("flop", "turn", None, None),
        P("flop", "turn"),
    )
    out_specs = (P("flop", None, None), P("flop", None, "turn", None, None), P())
    return jax.shard_map(
        per_device, mesh=mesh, in_specs=in_specs, out_specs=out_specs, check_vma=False
    )
```
